256 devices in a mesh: row: 8 (over x, y_hi), col: 32 (over y_lo, z, core).
Axes of the slice: x: 4, y: 4 (y_hi: 2, y_lo: 2; y = y_hi * 2 + y_lo), z: 8, core: 2. Of those that a mesh axis runs over, the one named last changes fastest.
Arguments:
- inputs: bfloat16 [768, 12288], P('col', 'row'), may hold values from -6 to 6
- weight_in: bfloat16 [12288, 24576], P('row', 'col'), may hold values from -0.0546875 to 0.0546875
- weight_out: bfloat16 [24576, 12288], P('col', 'row'), may hold values from -0.0390625 to 0.0390625
- cotangent: bfloat16 [768, 12288], P('col', 'row'), may hold values from -6 to 6
Outputs:
- output: bfloat16 [768, 12288], P('col', 'row')
- input_grad: bfloat16 [768, 12288], P('col', 'row')
- weight_in_grad: bfloat16 [12288, 24576], P('row', 'col')
- weight_out_grad: bfloat16 [24576, 12288], P('col', 'row')
The draws below stay inside these ranges and needn't reach their ends.
All inputs are finite; a program needn't handle non-finite values.
Results may differ from the reference program's by a relative error of at most 0.0049.
Values may be sent and summed in bfloat16 or wider, within the bound.
A program may use at most 128 MiB of HBM per device.

```python
import math
import jax
import jax.numpy as jnp

D = 12288
FF = 24576
TOKENS = 768


def level_of(stream_key, shape, split, least, largest):
    def one(position, shards_of):
        steps = jax.random.uniform(jax.random.fold_in(jax.random.fold_in(stream_key, 6), position), (shards_of,), jnp.float32, least / len(split), largest / len(split))
        return jnp.repeat(jnp.exp(steps), shape[position] // shards_of).reshape((-1,) + (1,) * (len(shape) - position - 1))

    factor_of = one(*split[0])
    for cut in split[1:]:
        factor_of = factor_of * one(*cut)
    return factor_of


def centred(rng, shape, width, reach, split=(), kind=jnp.bfloat16):
    result = jax.random.normal(rng, shape, jnp.float32) * width
    if len(split) > 0:
        result = level_of(rng, shape, split, -0.22, 0.18) * result
    return jnp.clip(result, min=-reach, max=reach).astype(kind)


def setup_inputs(seed: int = 0) -> dict:
    splits = jax.random.split(jax.random.key(seed), 5)
    inputs = centred(splits[0], (TOKENS, D), 1.0, 6.0, ((0, 32), (1, 8)))
    weight_in = centred(splits[1], (D, FF), D ** -0.5, 0.0546875, ((0, 8), (1, 32)))
    weight_out = centred(splits[2], (FF, D), FF ** -0.5, 0.0390625, ((0, 32), (1, 8)))
    cotangent = centred(splits[3], (TOKENS, D), 1.0, 6.0, ((0, 32), (1, 8)))
    return {"inputs": inputs, "weight_in": weight_in, "weight_out": weight_out, "cotangent": cotangent}


def gelu_value(preact):
    coeff = math.sqrt(2.0 / math.pi)
    inner = coeff * (preact + 0.044715 * preact * preact * preact)
    return 0.5 * preact * (1.0 + jnp.tanh(inner))

def gelu_slope(preact):
    coeff = math.sqrt(2.0 / math.pi)
    inner = coeff * (preact + 0.044715 * preact * preact * preact)
    tangent = jnp.tanh(inner)
    return 0.5 * (1.0 + tangent) + 0.5 * preact * (1.0 - tangent * tangent) * coeff * (1.0 + 3.0 * 0.044715 * preact * preact)

def reference(inputs, weight_in, weight_out, cotangent):
    preact = jnp.dot(inputs, weight_in, preferred_element_type=jnp.float32)
    upstream = jnp.dot(cotangent, weight_out.T, preferred_element_type=jnp.float32)
    hidden_act = gelu_value(preact).astype(jnp.bfloat16)
    hidden_grad = (upstream * gelu_slope(preact)).astype(jnp.bfloat16)
    output = jnp.dot(hidden_act, weight_out, preferred_element_type=jnp.float32).astype(jnp.bfloat16)
    input_grad = jnp.dot(hidden_grad, weight_in.T, preferred_element_type=jnp.float32).astype(jnp.bfloat16)
    grad_scale = float(TOKENS) ** (-0.5)
    block_width = FF // 8
    in_blocks = []
    out_blocks = []
    for block in range(8):
        lower = block * block_width
        upper = lower + block_width
        in_part = jnp.dot(inputs.T, hidden_grad[:, lower:upper], preferred_element_type=jnp.float32)
        in_blocks.append((in_part * grad_scale).astype(jnp.bfloat16))
        out_part = jnp.dot(hidden_act[:, lower:upper].T, cotangent, preferred_element_type=jnp.float32)
        out_blocks.append((out_part * grad_scale).astype(jnp.bfloat16))
    weight_in_grad = jnp.concatenate(in_blocks, axis=1)
    weight_out_grad = jnp.concatenate(out_blocks, axis=0)
    return (output, input_grad, weight_in_grad, weight_out_grad)
```

```python
import functools
import math

import jax
import jax.numpy as jnp
from jax import lax
from jax.experimental import pallas as pl
from jax.experimental.pallas import tpu as pltpu
from jax.sharding import PartitionSpec as P

NZ = 8
NX = 4
F32 = jnp.float32
BF16 = jnp.bfloat16
COEFF = math.sqrt(2.0 / math.pi)
LAST = 8


def gelu_value(preact):
    inner = COEFF * (preact + 0.044715 * preact * preact * preact)
    return 0.5 * preact * (1.0 + jnp.tanh(inner))


def gelu_slope(preact):
    inner = COEFF * (preact + 0.044715 * preact * preact * preact)
    tangent = jnp.tanh(inner)
    return 0.5 * (1.0 + tangent) + 0.5 * preact * (1.0 - tangent * tangent) * COEFF * (
        1.0 + 3.0 * 0.044715 * preact * preact
    )


def nn(a, b):
    return lax.dot_general(a, b, (((1,), (0,)), ((), ())), preferred_element_type=F32)


def nt(a, b):
    return lax.dot_general(a, b, (((1,), (1,)), ((), ())), preferred_element_type=F32)


def tn(a, b):
    return lax.dot_general(a, b, (((0,), (0,)), ((), ())), preferred_element_type=F32)


def kernel(
    scale,
    inputs, weight_in, weight_out, cotangent,
    out, igrad, wigrad, wograd,
    xp, xs, win, wout, pf, sx1, rx1, sx2, rx2, sy, ry, sc, rc, hid, otmp, oacc, sl, rl, sd, rd, grads, fin,
    loc_sem, w_ssem, w_rsem, xp_ssem, xp_rsem, ay_ssem, ay_rsem, a_ssem, a_rsem,
    x1_ssem, x1_rsem, x2_ssem, x2_rsem, y_ssem, y_rsem, c_ssem, c_rsem, g_ssem, g_rsem,
    l_ssem, l_rsem, d_ssem, d_rsem, o_lsem, o_ssem, o_rsem, f_lsem, f_ssem, f_rsem,
):
    row, col = lax.axis_index("row"), lax.axis_index("col")
    x, yh = row // 2, lax.rem(row, 2)
    yl, z, core = col // 16, lax.rem(col // 2, NZ), lax.rem(col, 2)
    other = 1 - core
    width = inputs.shape[1]
    half = width // 2
    quarter = width // 4
    twin = (row, col + 1 - 2 * core)
    ylo = (row, (1 - yl) * 16 + z * 2 + core)
    yhi = (x * 2 + 1 - yh, col)

    def zdev(step):
        return (row, yl * 16 + lax.rem(z + step + NZ, NZ) * 2 + core)

    def xdev(step):
        return (lax.rem(x + step + NX, NX) * 2 + yh, col)

    def xat(step):
        return lax.rem(x + step + NX, NX)

    def send(src, dst, ssem, rsem, dev):
        return pltpu.make_async_remote_copy(
            src_ref=src, dst_ref=dst, send_sem=ssem, recv_sem=rsem,
            device_id=dev, device_id_type=pl.DeviceIdType.MESH,
        )

    def arrived(dst, rsem):
        pltpu.make_async_copy(dst, dst, rsem).wait()

    @pl.when(core == 0)
    def _():
        pltpu.make_async_copy(weight_in, win.at[0], loc_sem.at[0]).start()
        pltpu.make_async_copy(inputs, xp.at[0], loc_sem.at[1]).start()

    @pl.when(core == 1)
    def _():
        pltpu.make_async_copy(weight_out, wout.at[1], loc_sem.at[0]).start()
        pltpu.make_async_copy(cotangent, xp.at[1], loc_sem.at[1]).start()

    barrier = pltpu.get_barrier_semaphore()
    for dev in (twin, ylo, yhi, zdev(1), zdev(-1), xdev(1), xdev(-1)):
        pl.semaphore_signal(barrier, inc=1, device_id=dev, device_id_type=pl.DeviceIdType.MESH)
    pl.semaphore_wait(barrier, 7)

    @pl.when(core == 0)
    def _():
        send(cotangent, xp.at[0], xp_ssem, xp_rsem, twin).start()
        send(weight_out, wout.at[0], w_ssem, w_rsem, twin).start()

    @pl.when(core == 1)
    def _():
        send(inputs, xp.at[1], xp_ssem, xp_rsem, twin).start()
        send(weight_in, win.at[1], w_ssem, w_rsem, twin).start()

    @pl.when(core == 0)
    def _():
        pltpu.make_async_copy(inputs, xp.at[0], loc_sem.at[1]).wait()
        send(inputs, xp.at[1], xp_ssem, xp_rsem, twin).wait_recv()

    @pl.when(core == 1)
    def _():
        pltpu.make_async_copy(cotangent, xp.at[1], loc_sem.at[1]).wait()
        send(cotangent, xp.at[0], xp_ssem, xp_rsem, twin).wait_recv()

    xs[z, yl] = jnp.concatenate([xp[0].astype(F32), xp[1].astype(F32)], axis=0).astype(BF16)

    def a_send(chunk, lo, way, step):
        block = xs.at[chunk, lo]
        dev = (row, yl * 16 + lax.rem(z + 1 - 2 * way + NZ, NZ) * 2 + core)
        return send(block, block, a_ssem.at[way, lo, step], a_rsem.at[way, lo, step], dev)

    own = xs.at[z, yl]
    send(own, own, ay_ssem, ay_rsem, ylo).start()
    a_send(z, yl, 0, 0).start()
    a_send(z, yl, 1, 0).start()
    theirs = xs.at[z, 1 - yl]
    send(theirs, theirs, ay_ssem, ay_rsem, ylo).wait_recv()
    a_send(z, 1 - yl, 0, 0).start()
    a_send(z, 1 - yl, 1, 0).start()

    @pl.when(core == 0)
    def _():
        pltpu.make_async_copy(weight_in, win.at[0], loc_sem.at[0]).wait()
        send(weight_in, win.at[1], w_ssem, w_rsem, twin).wait_recv()

    @pl.when(core == 1)
    def _():
        pltpu.make_async_copy(weight_out, wout.at[1], loc_sem.at[0]).wait()
        send(weight_out, wout.at[0], w_ssem, w_rsem, twin).wait_recv()

    def chunk_of(t):
        step = (t + 1) // 2
        return lax.rem(z + NZ + (1 - 2 * lax.rem(t, 2)) * step, NZ)

    def x1_send(c, way):
        return send(sx1.at[c, way], rx1.at[c, way], x1_ssem.at[c, way], x1_rsem.at[c, way], xdev(2 * way - 1))

    def x2_send(c, way, b):
        return send(
            sx2.at[c, way, b], rx2.at[c, way, b], x2_ssem.at[c, way, b], x2_rsem.at[c, way, b], xdev(2 * way - 1)
        )

    def y_send(c):
        return send(sy.at[c], ry.at[c], y_ssem.at[c], y_rsem.at[c], yhi)

    def c_send(c):
        return send(sc.at[c], rc.at[c], c_ssem.at[c], c_rsem.at[c], twin)

    def g_send(c, hb, b, slot, dev):
        piece = hid.at[c, hb, b]
        return send(piece, piece, g_ssem.at[c, slot], g_rsem.at[c, slot], dev)

    def l_send(c):
        return send(sl.at[c], rl.at[c], l_ssem.at[c], l_rsem.at[c], ylo)

    def during(it, lag, fn):
        t = it - lag

        @pl.when(jnp.logical_and(t >= 0, t < NZ))
        def _():
            fn(t, chunk_of(t))

    def stage_arrive(t, c):
        step = (t + 1) // 2

        @pl.when(t > 0)
        def _():
            for lo in range(2):
                way = jnp.where(t == NZ - 1, lo, 1 - lax.rem(t, 2))
                a_send(c, lo, way, step - 1).wait_recv()

                @pl.when(step < jnp.where(way == lo, 4, 3))
                def _():
                    a_send(c, lo, way, step).start()

    def stage_first(t, c):
        lhs = xs[c].reshape(96, width)

        def put(o, part):
            for j in range(2):
                pf[c, 2 * o + j] = part[:, j * quarter : (j + 1) * quarter].reshape(2, 48, quarter)

        @pl.when(core == 0)
        def _():
            for o in range(2):
                put(o, nn(lhs, win[o]))

        @pl.when(core == 1)
        def _():
            for o in range(2):
                put(o, nt(lhs, wout[o]))

        for way in range(2):
            sx1[c, way] = pf[c, xat(2), way].astype(BF16)
            x1_send(c, way).start()
        for way in range(2):
            sx2[c, way, 1 - way] = pf[c, xat(2 * way - 1), 1 - way].astype(BF16)
            x2_send(c, way, 1 - way).start()

    def stage_x2(t, c):
        for way in range(2):
            x1_send(c, way).wait_recv()
            sx2[c, way, way] = (pf[c, xat(2 * way - 1), way] + rx1[c, way].astype(F32)).astype(BF16)
            x2_send(c, way, way).start()

    def stage_y(t, c):
        for way in range(2):
            for b in range(2):
                x2_send(c, way, b).wait_recv()
        sy[c] = (
            pf[c, x, 1 - yh] + rx2[c, 0, 1 - yh].astype(F32) + rx2[c, 1, 1 - yh].astype(F32)
        )
        y_send(c).start()

    def stage_twin(t, c):
        y_send(c).wait_recv()
        sc[c] = pf[c, x, yh] + rx2[c, 0, yh].astype(F32) + rx2[c, 1, yh].astype(F32) + ry[c]
        c_send(c).start()

    def stage_gelu(t, c):
        c_send(c).wait_recv()

        @pl.when(core == 0)
        def _():
            hid[c, x, yh] = (rc[c] * gelu_slope(sc[c])).astype(BF16)

        @pl.when(core == 1)
        def _():
            hid[c, x, yh] = gelu_value(rc[c]).astype(BF16)

        g_send(c, x, yh, 0, yhi).start()
        g_send(c, x, yh, 1 + yh, xdev(1)).start()
        g_send(c, x, yh, 3 + yh, xdev(-1)).start()

    def forward(c, b):
        slot = 1 + 2 * b + b
        hb = xat(2 * b - 1)
        g_send(c, hb, b, slot, yhi).wait_recv()
        g_send(c, hb, b, 5 + b, xdev(1 - 2 * b)).start()

    def stage_spread(t, c):
        g_send(c, x, 1 - yh, 0, yhi).wait_recv()
        g_send(c, x, 1 - yh, 2 - yh, xdev(1)).start()
        g_send(c, x, 1 - yh, 4 - yh, xdev(-1)).start()
        forward(c, yh)

    def stage_spread2(t, c):
        forward(c, 1 - yh)

    def stage_second(t, c):
        g_send(c, xat(-1), 1, 2, yhi).wait_recv()
        g_send(c, xat(1), 0, 3, yhi).wait_recv()
        for b in range(2):
            g_send(c, xat(2), b, 5 + b, yhi).wait_recv()
        lhs = [
            jnp.concatenate([hid[c, 2 * o + j].reshape(96, quarter) for j in range(2)], axis=1) for o in range(2)
        ]

        @pl.when(core == 0)
        def _():
            otmp[...] = (nt(lhs[0], win[0]) + nt(lhs[1], win[1])).reshape(2, 48, width)

        @pl.when(core == 1)
        def _():
            otmp[...] = (nn(lhs[0], wout[0]) + nn(lhs[1], wout[1])).reshape(2, 48, width)

        sl[c] = otmp[1 - yl].astype(BF16)
        l_send(c).start()
        oacc[c] = otmp[yl]

    def stage_pair(t, c):
        l_send(c).wait_recv()
        oacc[c] += rl[c].astype(F32)

    stages = (
        stage_pair, stage_spread2, stage_spread, stage_gelu, stage_twin, stage_y, stage_x2, stage_arrive,
        stage_first, stage_second,
    )
    lags = (8, 6, 5, 4, 3, 2, 1, 0, 0, 7)

    def loop(it, carry):
        for fn, lag in zip(stages, lags):
            during(it, lag, fn)
        return carry

    lax.fori_loop(0, NZ + LAST, loop, 0)

    def grad_tile(o, i):
        @pl.when(core == 0)
        def _():
            lhs = xs[:, :, :, pl.ds(pl.multiple_of(i * quarter, 128), quarter)].reshape(NZ * 96, quarter)
            rhs = jnp.concatenate([hid[:, 2 * o + j].reshape(NZ * 96, quarter) for j in range(2)], axis=1)
            grads[o, i] = (tn(lhs, rhs) * scale).astype(BF16)

        @pl.when(core == 1)
        def _():
            lhs = hid[:, 2 * o + i // 2].reshape(NZ * 96, quarter)
            rhs = xs[:, :, :, pl.ds(pl.multiple_of(lax.rem(i, 2) * half, 128), half)].reshape(NZ * 96, half)
            grads[o, i] = (tn(lhs, rhs) * scale).astype(BF16)

    def grad_place(i):
        a = wigrad.at[pl.ds(pl.multiple_of(i * quarter, 128), quarter), :]
        b = wograd.at[
            pl.ds(pl.multiple_of((i // 2) * quarter, 128), quarter),
            pl.ds(pl.multiple_of(lax.rem(i, 2) * half, 128), half),
        ]
        return a, b

    def grad_send(i):
        a, b = grad_place(i)

        @pl.when(core == 0)
        def _():
            send(grads.at[1, i], a, o_ssem.at[i], o_rsem.at[i], twin).start()

        @pl.when(core == 1)
        def _():
            send(grads.at[0, i], b, o_ssem.at[i], o_rsem.at[i], twin).start()

    def grad_keep(i):
        a, b = grad_place(i)

        @pl.when(core == 0)
        def _():
            pltpu.make_async_copy(grads.at[0, i], a, o_lsem.at[i]).start()

        @pl.when(core == 1)
        def _():
            pltpu.make_async_copy(grads.at[1, i], b, o_lsem.at[i]).start()

    def grad_step(k):
        def one(i, carry):
            if k < 2:
                grad_tile(other, i)
                grad_send(i)
            else:
                grad_tile(core, i)
                grad_keep(i)
            return carry

        first = 2 * (k % 2)
        lax.fori_loop(first, first + 2, one, 0)

    streams = ((1, 0, 4), (1, half, 3), (-1, 0, 3), (-1, half, 4))

    def d_send(s, k):
        return send(sd.at[s, k], rd.at[s, k], d_ssem.at[s, k], d_rsem.at[s, k], zdev(streams[s][0]))

    for k in range(4):
        for s in (0, 3, 1, 2):
            sign, first, hops = streams[s]
            if k >= hops:
                continue
            dest = lax.rem(z + NZ + sign * (hops - k), NZ)
            value = oacc[dest, :, first : first + half]
            if k > 0:
                d_send(s, k - 1).wait_recv()
                value = value + rd[s, k - 1].astype(F32)
            sd[s, k] = value.astype(BF16)
            d_send(s, k).start()
        grad_step(k)

    for s in range(4):
        d_send(s, streams[s][2] - 1).wait_recv()
    total = oacc[z] + jnp.concatenate(
        [
            rd[0, 3].astype(F32) + rd[2, 2].astype(F32),
            rd[1, 2].astype(F32) + rd[3, 3].astype(F32),
        ],
        axis=1,
    )
    fin[0] = total[:24].astype(BF16)
    fin[1] = total[24:].astype(BF16)

    @pl.when(core == 0)
    def _():
        send(fin.at[1], igrad, f_ssem, f_rsem, twin).start()
        pltpu.make_async_copy(fin.at[0], igrad, f_lsem).start()

    @pl.when(core == 1)
    def _():
        send(fin.at[0], out, f_ssem, f_rsem, twin).start()
        pltpu.make_async_copy(fin.at[1], out, f_lsem).start()

    send(own, own, ay_ssem, ay_rsem, ylo).wait_send()
    for way in range(2):
        for lo in range(2):
            for step in range(4 if way == lo else 3):
                a_send(z, lo, way, step).wait_send()

    def drain(c, carry):
        for way in range(2):
            x1_send(c, way).wait_send()
            for b in range(2):
                x2_send(c, way, b).wait_send()
        y_send(c).wait_send()
        c_send(c).wait_send()
        for slot in range(7):
            g_send(c, x, yh, slot, yhi).wait_send()
        l_send(c).wait_send()
        return carry

    lax.fori_loop(0, NZ, drain, 0)
    for s in range(4):
        for k in range(streams[s][2]):
            d_send(s, k).wait_send()

    for c, mine, his, parcel, wbuf, slot, result, other_result, tokens in (
        (0, wigrad, wograd, weight_out, wout, 0, igrad, out, cotangent),
        (1, wograd, wigrad, weight_in, win, 1, out, igrad, inputs),
    ):
        @pl.when(core == c)
        def _():
            send(tokens, xp.at[c], xp_ssem, xp_rsem, twin).wait_send()
            send(parcel, wbuf.at[slot], w_ssem, w_rsem, twin).wait_send()
            for i in range(4):
                a, b = grad_place(i)
                keep, take = (a, b) if c == 0 else (b, a)
                pltpu.make_async_copy(grads.at[c, i], keep, o_lsem.at[i]).wait()
                send(grads.at[1 - c, i], keep, o_ssem.at[i], o_rsem.at[i], twin).wait_send()
                send(grads.at[c, i], take, o_ssem.at[i], o_rsem.at[i], twin).wait_recv()
            pltpu.make_async_copy(fin.at[c], result, f_lsem).wait()
            send(fin.at[1 - c], result, f_ssem, f_rsem, twin).wait_send()
            send(fin.at[c], other_result, f_ssem, f_rsem, twin).wait_recv()


def body(inputs, weight_in, weight_out, cotangent):
    tokens, width = inputs.shape
    hidden = weight_in.shape[1]
    quarter = width // 4
    total_tokens = tokens * 32
    dma = pltpu.SemaphoreType.DMA
    vmem = pltpu.VMEM
    piece = (48, quarter)
    scratch = [
        vmem((2, tokens, width), BF16),
        vmem((NZ, 2, 48, width), BF16),
        vmem((2, width, hidden), BF16),
        vmem((2, hidden, width), BF16),
        vmem((NZ, 4, 2) + piece, F32),
        vmem((NZ, 2) + piece, BF16),
        vmem((NZ, 2) + piece, BF16),
        vmem((NZ, 2, 2) + piece, BF16),
        vmem((NZ, 2, 2) + piece, BF16),
        vmem((NZ,) + piece, F32),
        vmem((NZ,) + piece, F32),
        vmem((NZ,) + piece, F32),
        vmem((NZ,) + piece, F32),
        vmem((NZ, 4, 2) + piece, BF16),
        vmem((2, 48, width), F32),
        vmem((NZ, 48, width), F32),
        vmem((NZ, 48, width), BF16),
        vmem((NZ, 48, width), BF16),
        vmem((4, 4, 48, width // 2), BF16),
        vmem((4, 4, 48, width // 2), BF16),
        vmem((2, 4, quarter, width // 2), BF16),
        vmem((2, tokens, width), BF16),
        dma((2,)),
        dma, dma, dma, dma, dma, dma,
        dma((2, 2, 4)), dma((2, 2, 4)),
        dma((NZ, 2)), dma((NZ, 2)),
        dma((NZ, 2, 2)), dma((NZ, 2, 2)),
        dma((NZ,)), dma((NZ,)),
        dma((NZ,)), dma((NZ,)),
        dma((NZ, 7)), dma((NZ, 7)),
        dma((NZ,)), dma((NZ,)),
        dma((4, 4)), dma((4, 4)),
        dma((4,)), dma((4,)), dma((4,)),
        dma, dma, dma,
    ]
    shapes = (inputs.shape, cotangent.shape, weight_in.shape, weight_out.shape)
    return pl.pallas_call(
        functools.partial(kernel, float(total_tokens) ** (-0.5)),
        out_shape=tuple(jax.ShapeDtypeStruct(s, BF16) for s in shapes),
        in_specs=[pl.BlockSpec(memory_space=pl.ANY)] * 4,
        out_specs=tuple([pl.BlockSpec(memory_space=pl.ANY)] * 4),
        scratch_shapes=scratch,
        compiler_params=pltpu.CompilerParams(
            collective_id=0, has_side_effects=True, vmem_limit_bytes=58 * 1024 * 1024
        ),
        name="block",
    )(inputs, weight_in, weight_out, cotangent)


def solution(mesh):
    in_specs = (P("col", "row"), P("row", "col"), P("col", "row"), P("col", "row"))
    out_specs = (P("col", "row"), P("col", "row"), P("row", "col"), P("col", "row"))
    return jax.shard_map(body, mesh=mesh, in_specs=in_specs, out_specs=out_specs, check_vma=False)
```

```python
import functools
import math

import jax
import jax.numpy as jnp
from jax import lax
from jax.experimental import pallas as pl
from jax.experimental.pallas import tpu as pltpu
from jax.sharding import PartitionSpec as P

NZ = 8
NX = 4
F32 = jnp.float32
BF16 = jnp.bfloat16
COEFF = math.sqrt(2.0 / math.pi)
LAST = 4
GATHER_BOTH = (True, True)
REDUCE_BOTH = (False, False)


def gelu_value(preact):
    inner = COEFF * (preact + 0.044715 * preact * preact * preact)
    return 0.5 * preact * (1.0 + jnp.tanh(inner))


def gelu_slope(preact):
    inner = COEFF * (preact + 0.044715 * preact * preact * preact)
    tangent = jnp.tanh(inner)
    return 0.5 * (1.0 + tangent) + 0.5 * preact * (1.0 - tangent * tangent) * COEFF * (
        1.0 + 3.0 * 0.044715 * preact * preact
    )


def nn(a, b):
    return lax.dot_general(a, b, (((1,), (0,)), ((), ())), preferred_element_type=F32)


def nt(a, b):
    return lax.dot_general(a, b, (((1,), (1,)), ((), ())), preferred_element_type=F32)


def tn(a, b):
    return lax.dot_general(a, b, (((0,), (0,)), ((), ())), preferred_element_type=F32)


def kernel(
    scale,
    inputs, weight_in, weight_out, cotangent,
    out, igrad, wigrad, wograd,
    xp, xs, win, wout, pf, sx1, rx1, sx2, rx2, sy, ry, sc, rc, hid, oacc, sl, rl, sd, rd, se, re, grads, fin,
    loc_sem, w_ssem, w_rsem, xp_ssem, xp_rsem, ay_ssem, ay_rsem, a_ssem, a_rsem,
    x1_ssem, x1_rsem, x2_ssem, x2_rsem, y_ssem, y_rsem, c_ssem, c_rsem, g_ssem, g_rsem,
    l_ssem, l_rsem, d_ssem, d_rsem, e_ssem, e_rsem, o_lsem, o_ssem, o_rsem, f_lsem, f_ssem, f_rsem,
):
    row, col = lax.axis_index("row"), lax.axis_index("col")
    x, yh = row // 2, lax.rem(row, 2)
    yl, z, core = col // 16, lax.rem(col // 2, NZ), lax.rem(col, 2)
    other = 1 - core
    width = inputs.shape[1]
    half = width // 2
    quarter = width // 4
    twin = (row, col + 1 - 2 * core)
    ylo = (row, (1 - yl) * 16 + z * 2 + core)
    yhi = (x * 2 + 1 - yh, col)

    def zdev(step):
        return (row, yl * 16 + lax.rem(z + step + NZ, NZ) * 2 + core)

    def xdev(step):
        return (lax.rem(x + step + NX, NX) * 2 + yh, col)

    def xat(step):
        return lax.rem(x + step + NX, NX)

    def send(src, dst, ssem, rsem, dev):
        return pltpu.make_async_remote_copy(
            src_ref=src, dst_ref=dst, send_sem=ssem, recv_sem=rsem,
            device_id=dev, device_id_type=pl.DeviceIdType.MESH,
        )

    @pl.when(core == 0)
    def _():
        pltpu.make_async_copy(weight_in, win.at[0], loc_sem.at[0]).start()
        pltpu.make_async_copy(inputs, xp.at[0], loc_sem.at[1]).start()

    @pl.when(core == 1)
    def _():
        pltpu.make_async_copy(weight_out, wout.at[1], loc_sem.at[0]).start()
        pltpu.make_async_copy(cotangent, xp.at[1], loc_sem.at[1]).start()

    barrier = pltpu.get_barrier_semaphore()
    for dev in (twin, ylo, yhi, zdev(1), zdev(-1), xdev(1), xdev(-1)):
        pl.semaphore_signal(barrier, inc=1, device_id=dev, device_id_type=pl.DeviceIdType.MESH)
    pl.semaphore_wait(barrier, 7)

    @pl.when(core == 0)
    def _():
        send(cotangent, xp.at[0], xp_ssem, xp_rsem, twin).start()
        send(weight_out, wout.at[0], w_ssem, w_rsem, twin).start()

    @pl.when(core == 1)
    def _():
        send(inputs, xp.at[1], xp_ssem, xp_rsem, twin).start()
        send(weight_in, win.at[1], w_ssem, w_rsem, twin).start()

    @pl.when(core == 0)
    def _():
        pltpu.make_async_copy(inputs, xp.at[0], loc_sem.at[1]).wait()
        send(inputs, xp.at[1], xp_ssem, xp_rsem, twin).wait_recv()

    @pl.when(core == 1)
    def _():
        pltpu.make_async_copy(cotangent, xp.at[1], loc_sem.at[1]).wait()
        send(cotangent, xp.at[0], xp_ssem, xp_rsem, twin).wait_recv()

    block = jnp.concatenate([xp[0].astype(F32), xp[1].astype(F32)], axis=0).astype(BF16)
    for h in range(2):
        xs[z, yl, h] = block[:, h * half : (h + 1) * half]

    def ay_send(chunk, lo, h):
        piece = xs.at[chunk, lo, h]
        return send(piece, piece, ay_ssem.at[chunk, h], ay_rsem.at[chunk, h], ylo)

    def a_send(chunk, lo, h, way, step):
        piece = xs.at[chunk, lo, h]
        dev = (row, yl * 16 + lax.rem(z + 1 - 2 * way + NZ, NZ) * 2 + core)
        return send(piece, piece, a_ssem.at[way, lo, h, step], a_rsem.at[way, lo, h, step], dev)

    for h in range(2):
        ay_send(z, yl, h).start()
        for way in range(2):
            a_send(z, yl, h, way, 0).start()
    for h in range(2):
        ay_send(z, 1 - yl, h).wait_recv()
        if GATHER_BOTH[h]:
            for way in range(2):
                a_send(z, 1 - yl, h, way, 0).start()

    @pl.when(core == 0)
    def _():
        pltpu.make_async_copy(weight_in, win.at[0], loc_sem.at[0]).wait()
        send(weight_in, win.at[1], w_ssem, w_rsem, twin).wait_recv()

    @pl.when(core == 1)
    def _():
        pltpu.make_async_copy(weight_out, wout.at[1], loc_sem.at[0]).wait()
        send(weight_out, wout.at[0], w_ssem, w_rsem, twin).wait_recv()

    def chunk_of(t):
        step = (t + 1) // 2
        return lax.rem(z + NZ + (1 - 2 * lax.rem(t, 2)) * step, NZ)

    def x1_send(c, way):
        return send(sx1.at[c, way], rx1.at[c, way], x1_ssem.at[c, way], x1_rsem.at[c, way], xdev(2 * way - 1))

    def x2_send(c, way, b):
        return send(
            sx2.at[c, way, b], rx2.at[c, way, b], x2_ssem.at[c, way, b], x2_rsem.at[c, way, b], xdev(2 * way - 1)
        )

    def y_send(c):
        return send(sy.at[c], ry.at[c], y_ssem.at[c], y_rsem.at[c], yhi)

    def c_send(c):
        return send(sc.at[c], rc.at[c], c_ssem.at[c], c_rsem.at[c], twin)

    def g_send(c, hb, b, slot, dev):
        piece = hid.at[c, hb, b]
        return send(piece, piece, g_ssem.at[c, slot], g_rsem.at[c, slot], dev)

    def l_send(c, h):
        return send(sl.at[c, h], rl.at[c, h], l_ssem.at[c, h], l_rsem.at[c, h], ylo)

    def during(it, lag, fn):
        t = 2 * (it - lag)

        @pl.when(jnp.logical_and(t > 0, t <= NZ))
        def _():
            fn(t - 1, chunk_of(t - 1))

        @pl.when(jnp.logical_and(t >= 0, t < NZ))
        def _():
            fn(t, chunk_of(t))

    def stage_arrive(t, c):
        step = (t + 1) // 2

        def take(lo, h, four):
            way = jnp.where(t == NZ - 1, four, 1 - lax.rem(t, 2))
            a_send(c, lo, h, way, step - 1).wait_recv()

            @pl.when(step < jnp.where(way == four, 4, 3))
            def _():
                a_send(c, lo, h, way, step).start()

        @pl.when(t > 0)
        def _():
            for h in range(2):
                if GATHER_BOTH[h]:
                    take(0, h, 0)
                    take(1, h, 1)
                else:
                    take(yl, h, 0)
                    ay_send(c, yl, h).start()

    def stage_first(t, c):
        @pl.when(t > 0)
        def _():
            for h in range(2):
                if not GATHER_BOTH[h]:
                    ay_send(c, 1 - yl, h).wait_recv()

        lhs = jnp.concatenate([xs[c, :, h].reshape(96, half) for h in range(2)], axis=1)

        def put(o, part):
            for j in range(2):
                pf[c, 2 * o + j] = part[:, j * quarter : (j + 1) * quarter].reshape(2, 48, quarter)

        @pl.when(core == 0)
        def _():
            for o in range(2):
                put(o, nn(lhs, win[o]))

        @pl.when(core == 1)
        def _():
            for o in range(2):
                put(o, nt(lhs, wout[o]))

        for way in range(2):
            sx1[c, way] = pf[c, xat(2), way].astype(BF16)
            x1_send(c, way).start()
        for way in range(2):
            sx2[c, way, 1 - way] = pf[c, xat(2 * way - 1), 1 - way].astype(BF16)
            x2_send(c, way, 1 - way).start()

    def stage_x2(t, c):
        for way in range(2):
            x1_send(c, way).wait_recv()
            sx2[c, way, way] = (pf[c, xat(2 * way - 1), way] + rx1[c, way].astype(F32)).astype(BF16)
            x2_send(c, way, way).start()

    def stage_y(t, c):
        for way in range(2):
            for b in range(2):
                x2_send(c, way, b).wait_recv()
        sy[c] = (
            pf[c, x, 1 - yh] + rx2[c, 0, 1 - yh].astype(F32) + rx2[c, 1, 1 - yh].astype(F32)
        )
        y_send(c).start()

    def stage_twin(t, c):
        y_send(c).wait_recv()
        sc[c] = pf[c, x, yh] + rx2[c, 0, yh].astype(F32) + rx2[c, 1, yh].astype(F32) + ry[c]
        c_send(c).start()

    def stage_gelu(t, c):
        c_send(c).wait_recv()

        @pl.when(core == 0)
        def _():
            hid[c, x, yh] = (rc[c] * gelu_slope(sc[c])).astype(BF16)

        @pl.when(core == 1)
        def _():
            hid[c, x, yh] = gelu_value(rc[c]).astype(BF16)

        g_send(c, x, yh, 0, yhi).start()
        g_send(c, x, yh, 1 + yh, xdev(1)).start()
        g_send(c, x, yh, 3 + yh, xdev(-1)).start()

    def forward(c, b):
        slot = 1 + 2 * b + b
        hb = xat(2 * b - 1)
        g_send(c, hb, b, slot, yhi).wait_recv()
        g_send(c, hb, b, 5 + b, xdev(1 - 2 * b)).start()

    def stage_spread(t, c):
        g_send(c, x, 1 - yh, 0, yhi).wait_recv()
        g_send(c, x, 1 - yh, 2 - yh, xdev(1)).start()
        g_send(c, x, 1 - yh, 4 - yh, xdev(-1)).start()
        forward(c, yh)

    def stage_spread2(t, c):
        forward(c, 1 - yh)

    def stage_second(t, c):
        g_send(c, xat(-1), 1, 2, yhi).wait_recv()
        g_send(c, xat(1), 0, 3, yhi).wait_recv()
        for b in range(2):
            g_send(c, xat(2), b, 5 + b, yhi).wait_recv()
        lhs = [
            jnp.concatenate([hid[c, 2 * o + j].reshape(96, quarter) for j in range(2)], axis=1) for o in range(2)
        ]

        @pl.when(core == 0)
        def _():
            oacc[c] = (nt(lhs[0], win[0]) + nt(lhs[1], win[1])).reshape(2, 48, width)

        @pl.when(core == 1)
        def _():
            oacc[c] = (nn(lhs[0], wout[0]) + nn(lhs[1], wout[1])).reshape(2, 48, width)

        for h in range(2):
            if not REDUCE_BOTH[h]:
                sl[c, h] = oacc[c, 1 - yl, :, h * half : (h + 1) * half].astype(BF16)
                l_send(c, h).start()

    def stage_pair(t, c):
        for h in range(2):
            if not REDUCE_BOTH[h]:
                l_send(c, h).wait_recv()
                oacc[c, yl, :, h * half : (h + 1) * half] += rl[c, h].astype(F32)

    stages = (
        (stage_first, 0), (stage_y, 1), (stage_spread, 2), (stage_second, 3),
        (stage_x2, 0), (stage_twin, 1), (stage_spread2, 2), (stage_pair, 4), (stage_gelu, 1), (stage_arrive, -1),
    )

    def loop(it, carry):
        for fn, lag in stages:
            during(it, lag, fn)
        return carry

    lax.fori_loop(0, NZ // 2 + 1 + LAST, loop, 0)

    def grad_tile(o, i):
        @pl.when(core == 0)
        def _():
            lhs = xs[:, :, i // 2, :, pl.ds(pl.multiple_of(lax.rem(i, 2) * quarter, 128), quarter)]
            lhs = lhs.reshape(NZ * 96, quarter)
            rhs = jnp.concatenate([hid[:, 2 * o + j].reshape(NZ * 96, quarter) for j in range(2)], axis=1)
            grads[o, i] = (tn(lhs, rhs) * scale).astype(BF16)

        @pl.when(core == 1)
        def _():
            lhs = hid[:, 2 * o + i // 2].reshape(NZ * 96, quarter)
            rhs = xs[:, :, lax.rem(i, 2)].reshape(NZ * 96, half)
            grads[o, i] = (tn(lhs, rhs) * scale).astype(BF16)

    def grad_place(i):
        a = wigrad.at[pl.ds(pl.multiple_of(i * quarter, 128), quarter), :]
        b = wograd.at[
            pl.ds(pl.multiple_of((i // 2) * quarter, 128), quarter),
            pl.ds(pl.multiple_of(lax.rem(i, 2) * half, 128), half),
        ]
        return a, b

    def grad_send(i):
        a, b = grad_place(i)

        @pl.when(core == 0)
        def _():
            send(grads.at[1, i], a, o_ssem.at[i], o_rsem.at[i], twin).start()

        @pl.when(core == 1)
        def _():
            send(grads.at[0, i], b, o_ssem.at[i], o_rsem.at[i], twin).start()

    def grad_keep(i):
        a, b = grad_place(i)

        @pl.when(core == 0)
        def _():
            pltpu.make_async_copy(grads.at[0, i], a, o_lsem.at[i]).start()

        @pl.when(core == 1)
        def _():
            pltpu.make_async_copy(grads.at[1, i], b, o_lsem.at[i]).start()

    def grad_step(k):
        def one(i, carry):
            if k < 2:
                grad_tile(other, i)
                grad_send(i)
            else:
                grad_tile(core, i)
                grad_keep(i)
            return carry

        first = 2 * (k % 2)
        lax.fori_loop(first, first + 2, one, 0)

    streams = []
    for h in range(2):
        for far in ((True, False) if REDUCE_BOTH[h] else (False,)):
            longer = 1 if (h == 0) == far else -1
            for sign in (1, -1):
                streams.append((sign, h, far, 4 if sign == longer else 3))
    order = sorted(range(len(streams)), key=lambda i: (not streams[i][2], -streams[i][3]))

    def target(far):
        return 1 - yl if far else yl

    def d_send(s, k):
        return send(sd.at[s, k], rd.at[s, k], d_ssem.at[s, k], d_rsem.at[s, k], zdev(streams[s][0]))

    def e_send(h):
        return send(se.at[h], re.at[h], e_ssem.at[h], e_rsem.at[h], ylo)

    for k in range(4):
        for s in order:
            sign, h, far, hops = streams[s]
            if k >= hops:
                continue
            dest = lax.rem(z + NZ + sign * (hops - k), NZ)
            value = oacc[dest, target(far), :, h * half : (h + 1) * half]
            if k > 0:
                d_send(s, k - 1).wait_recv()
                value = value + rd[s, k - 1].astype(F32)
            sd[s, k] = value.astype(BF16)
            d_send(s, k).start()
        grad_step(k)

    def ring_total(h, far):
        value = oacc[z, target(far), :, h * half : (h + 1) * half]
        for s, (_, at, away, hops) in enumerate(streams):
            if at == h and away == far:
                d_send(s, hops - 1).wait_recv()
                value = value + rd[s, hops - 1].astype(F32)
        return value

    for h in range(2):
        if REDUCE_BOTH[h]:
            se[h] = ring_total(h, True)
            e_send(h).start()
    parts = [ring_total(h, False) for h in range(2)]
    for h in range(2):
        if REDUCE_BOTH[h]:
            e_send(h).wait_recv()
            parts[h] = parts[h] + re[h]
    total = jnp.concatenate(parts, axis=1)
    fin[0] = total[:24].astype(BF16)
    fin[1] = total[24:].astype(BF16)

    @pl.when(core == 0)
    def _():
        send(fin.at[1], igrad, f_ssem, f_rsem, twin).start()
        pltpu.make_async_copy(fin.at[0], igrad, f_lsem).start()

    @pl.when(core == 1)
    def _():
        send(fin.at[0], out, f_ssem, f_rsem, twin).start()
        pltpu.make_async_copy(fin.at[1], out, f_lsem).start()

    for way in range(2):
        for h in range(2):
            for lo, four in (((0, 0), (1, 1)) if GATHER_BOTH[h] else ((yl, 0),)):
                for step in range(4 if way == four else 3):
                    a_send(z, lo, h, way, step).wait_send()
    for h in range(2):
        if GATHER_BOTH[h]:
            ay_send(z, yl, h).wait_send()
        if REDUCE_BOTH[h]:
            e_send(h).wait_send()

    def drain(c, carry):
        for way in range(2):
            x1_send(c, way).wait_send()
            for b in range(2):
                x2_send(c, way, b).wait_send()
        y_send(c).wait_send()
        c_send(c).wait_send()
        for slot in range(7):
            g_send(c, x, yh, slot, yhi).wait_send()
        for h in range(2):
            if not GATHER_BOTH[h]:
                ay_send(c, yl, h).wait_send()
            if not REDUCE_BOTH[h]:
                l_send(c, h).wait_send()
        return carry

    lax.fori_loop(0, NZ, drain, 0)
    for s in range(len(streams)):
        for k in range(streams[s][3]):
            d_send(s, k).wait_send()

    for c, mine, his, parcel, wbuf, slot, result, other_result, tokens in (
        (0, wigrad, wograd, weight_out, wout, 0, igrad, out, cotangent),
        (1, wograd, wigrad, weight_in, win, 1, out, igrad, inputs),
    ):
        @pl.when(core == c)
        def _():
            send(tokens, xp.at[c], xp_ssem, xp_rsem, twin).wait_send()
            send(parcel, wbuf.at[slot], w_ssem, w_rsem, twin).wait_send()
            for i in range(4):
                a, b = grad_place(i)
                keep, take = (a, b) if c == 0 else (b, a)
                pltpu.make_async_copy(grads.at[c, i], keep, o_lsem.at[i]).wait()
                send(grads.at[1 - c, i], keep, o_ssem.at[i], o_rsem.at[i], twin).wait_send()
                send(grads.at[c, i], take, o_ssem.at[i], o_rsem.at[i], twin).wait_recv()
            pltpu.make_async_copy(fin.at[c], result, f_lsem).wait()
            send(fin.at[1 - c], result, f_ssem, f_rsem, twin).wait_send()
            send(fin.at[c], other_result, f_ssem, f_rsem, twin).wait_recv()


def body(inputs, weight_in, weight_out, cotangent):
    tokens, width = inputs.shape
    hidden = weight_in.shape[1]
    quarter = width // 4
    total_tokens = tokens * 32
    dma = pltpu.SemaphoreType.DMA
    vmem = pltpu.VMEM
    piece = (48, quarter)
    scratch = [
        vmem((2, tokens, width), BF16),
        vmem((NZ, 2, 2, 48, width // 2), BF16),
        vmem((2, width, hidden), BF16),
        vmem((2, hidden, width), BF16),
        vmem((NZ, 4, 2) + piece, F32),
        vmem((NZ, 2) + piece, BF16),
        vmem((NZ, 2) + piece, BF16),
        vmem((NZ, 2, 2) + piece, BF16),
        vmem((NZ, 2, 2) + piece, BF16),
        vmem((NZ,) + piece, F32),
        vmem((NZ,) + piece, F32),
        vmem((NZ,) + piece, F32),
        vmem((NZ,) + piece, F32),
        vmem((NZ, 4, 2) + piece, BF16),
        vmem((NZ, 2, 48, width), F32),
        vmem((NZ, 2, 48, width // 2), BF16),
        vmem((NZ, 2, 48, width // 2), BF16),
        vmem((8, 4, 48, width // 2), BF16),
        vmem((8, 4, 48, width // 2), BF16),
        vmem((2, 48, width // 2), F32),
        vmem((2, 48, width // 2), F32),
        vmem((2, 4, quarter, width // 2), BF16),
        vmem((2, tokens, width), BF16),
        dma((2,)),
        dma, dma, dma, dma,
        dma((NZ, 2)), dma((NZ, 2)),
        dma((2, 2, 2, 4)), dma((2, 2, 2, 4)),
        dma((NZ, 2)), dma((NZ, 2)),
        dma((NZ, 2, 2)), dma((NZ, 2, 2)),
        dma((NZ,)), dma((NZ,)),
        dma((NZ,)), dma((NZ,)),
        dma((NZ, 7)), dma((NZ, 7)),
        dma((NZ, 2)), dma((NZ, 2)),
        dma((8, 4)), dma((8, 4)),
        dma((2,)), dma((2,)),
        dma((4,)), dma((4,)), dma((4,)),
        dma, dma, dma,
    ]
    shapes = (inputs.shape, cotangent.shape, weight_in.shape, weight_out.shape)
    return pl.pallas_call(
        functools.partial(kernel, float(total_tokens) ** (-0.5)),
        out_shape=tuple(jax.ShapeDtypeStruct(s, BF16) for s in shapes),
        in_specs=[pl.BlockSpec(memory_space=pl.ANY)] * 4,
        out_specs=tuple([pl.BlockSpec(memory_space=pl.ANY)] * 4),
        scratch_shapes=scratch,
        compiler_params=pltpu.CompilerParams(
            collective_id=0, has_side_effects=True, vmem_limit_bytes=58 * 1024 * 1024
        ),
        name="block",
    )(inputs, weight_in, weight_out, cotangent)


def solution(mesh):
    in_specs = (P("col", "row"), P("row", "col"), P("col", "row"), P("col", "row"))
    out_specs = (P("col", "row"), P("col", "row"), P("row", "col"), P("col", "row"))
    return jax.shard_map(body, mesh=mesh, in_specs=in_specs, out_specs=out_specs, check_vma=False)
```

```python
import functools
import math

import jax
import jax.numpy as jnp
from jax import lax
from jax.experimental import pallas as pl
from jax.experimental.pallas import tpu as pltpu
from jax.sharding import PartitionSpec as P

NZ = 8
NX = 4
F32 = jnp.float32
BF16 = jnp.bfloat16
COEFF = math.sqrt(2.0 / math.pi)
LAST = 3
REDUCE_BOTH = (True, False)


def gelu_value(preact):
    inner = COEFF * (preact + 0.044715 * preact * preact * preact)
    return 0.5 * preact * (1.0 + jnp.tanh(inner))


def gelu_slope(preact):
    inner = COEFF * (preact + 0.044715 * preact * preact * preact)
    tangent = jnp.tanh(inner)
    return 0.5 * (1.0 + tangent) + 0.5 * preact * (1.0 - tangent * tangent) * COEFF * (
        1.0 + 3.0 * 0.044715 * preact * preact
    )


def nn(a, b):
    return lax.dot_general(a, b, (((1,), (0,)), ((), ())), preferred_element_type=F32)


def nt(a, b):
    return lax.dot_general(a, b, (((1,), (1,)), ((), ())), preferred_element_type=F32)


def tn(a, b):
    return lax.dot_general(a, b, (((0,), (0,)), ((), ())), preferred_element_type=F32)


def kernel(
    scale,
    inputs, weight_in, weight_out, cotangent,
    out, igrad, wigrad, wograd,
    xp, xs, win, wout, pf, sx1, rx1, sx2, rx2, sy, ry, sc, rc, hid, oacc, sl, rl, sd, rd, se, re, grads, fin,
    loc_sem, w_ssem, w_rsem, xp_ssem, xp_rsem, a_ssem, a_rsem,
    x1_ssem, x1_rsem, x2_ssem, x2_rsem, y_ssem, y_rsem, c_ssem, c_rsem, g_ssem, g_rsem,
    l_ssem, l_rsem, d_ssem, d_rsem, e_ssem, e_rsem, o_lsem, o_ssem, o_rsem, f_lsem, f_ssem, f_rsem,
):
    row, col = lax.axis_index("row"), lax.axis_index("col")
    x, yh = row // 2, lax.rem(row, 2)
    yl, z, core = col // 16, lax.rem(col // 2, NZ), lax.rem(col, 2)
    other = 1 - core
    width = inputs.shape[1]
    half = width // 2
    quarter = width // 4
    twin = (row, col + 1 - 2 * core)
    ylo = (row, (1 - yl) * 16 + z * 2 + core)
    yhi = (x * 2 + 1 - yh, col)
    ylo_twin = (row, (1 - yl) * 16 + z * 2 + other)

    def zdev(step):
        return (row, yl * 16 + lax.rem(z + step + NZ, NZ) * 2 + core)

    def xdev(step):
        return (lax.rem(x + step + NX, NX) * 2 + yh, col)

    def xat(step):
        return lax.rem(x + step + NX, NX)

    def send(src, dst, ssem, rsem, dev):
        return pltpu.make_async_remote_copy(
            src_ref=src, dst_ref=dst, send_sem=ssem, recv_sem=rsem,
            device_id=dev, device_id_type=pl.DeviceIdType.MESH,
        )

    @pl.when(core == 0)
    def _():
        pltpu.make_async_copy(weight_in, win.at[0], loc_sem.at[0]).start()
        pltpu.make_async_copy(inputs, xp.at[yl, 0], loc_sem.at[1]).start()

    @pl.when(core == 1)
    def _():
        pltpu.make_async_copy(weight_out, wout.at[1], loc_sem.at[0]).start()
        pltpu.make_async_copy(cotangent, xp.at[yl, 1], loc_sem.at[1]).start()

    barrier = pltpu.get_barrier_semaphore()
    for dev in (twin, ylo, ylo_twin, yhi, zdev(1), zdev(-1), xdev(1), xdev(-1)):
        pl.semaphore_signal(barrier, inc=1, device_id=dev, device_id_type=pl.DeviceIdType.MESH)
    pl.semaphore_wait(barrier, 8)

    def token_sends(c, mine, his):
        slot = xp.at[yl, c]
        return (
            send(his, slot, xp_ssem.at[0], xp_rsem.at[0], twin),
            send(mine, slot, xp_ssem.at[1], xp_rsem.at[1], ylo),
            send(his, slot, xp_ssem.at[2], xp_rsem.at[2], ylo_twin),
        )

    @pl.when(core == 0)
    def _():
        for copy in token_sends(0, inputs, cotangent):
            copy.start()
        send(weight_out, wout.at[0], w_ssem, w_rsem, twin).start()

    @pl.when(core == 1)
    def _():
        for copy in token_sends(1, cotangent, inputs):
            copy.start()
        send(weight_in, win.at[1], w_ssem, w_rsem, twin).start()

    @pl.when(core == 0)
    def _():
        pltpu.make_async_copy(inputs, xp.at[yl, 0], loc_sem.at[1]).wait()

    @pl.when(core == 1)
    def _():
        pltpu.make_async_copy(cotangent, xp.at[yl, 1], loc_sem.at[1]).wait()

    def build(lo):
        block = jnp.concatenate([xp[lo, 0].astype(F32), xp[lo, 1].astype(F32)], axis=0).astype(BF16)
        for h in range(2):
            xs[z, lo, h] = block[:, h * half : (h + 1) * half]

    def a_send(chunk, lo, h, way, step):
        piece = xs.at[chunk, lo, h]
        dev = (row, yl * 16 + lax.rem(z + 1 - 2 * way + NZ, NZ) * 2 + core)
        return send(piece, piece, a_ssem.at[way, lo, h, step], a_rsem.at[way, lo, h, step], dev)

    send(inputs, xp.at[yl, other], xp_ssem.at[0], xp_rsem.at[0], twin).wait_recv()
    build(yl)
    for h in range(2):
        for way in range(2):
            a_send(z, yl, h, way, 0).start()
    send(inputs, xp.at[1 - yl, core], xp_ssem.at[1], xp_rsem.at[1], ylo).wait_recv()
    send(inputs, xp.at[1 - yl, other], xp_ssem.at[2], xp_rsem.at[2], ylo_twin).wait_recv()
    build(1 - yl)
    for h in range(2):
        for way in range(2):
            a_send(z, 1 - yl, h, way, 0).start()

    @pl.when(core == 0)
    def _():
        pltpu.make_async_copy(weight_in, win.at[0], loc_sem.at[0]).wait()
        send(weight_in, win.at[1], w_ssem, w_rsem, twin).wait_recv()

    @pl.when(core == 1)
    def _():
        pltpu.make_async_copy(weight_out, wout.at[1], loc_sem.at[0]).wait()
        send(weight_out, wout.at[0], w_ssem, w_rsem, twin).wait_recv()

    def chunk_of(t):
        step = (t + 1) // 2
        return lax.rem(z + NZ + (1 - 2 * lax.rem(t, 2)) * step, NZ)

    def x1_send(c, way):
        return send(sx1.at[c, way], rx1.at[c, way], x1_ssem.at[c, way], x1_rsem.at[c, way], xdev(2 * way - 1))

    def x2_send(c, way, b):
        return send(
            sx2.at[c, way, b], rx2.at[c, way, b], x2_ssem.at[c, way, b], x2_rsem.at[c, way, b], xdev(2 * way - 1)
        )

    def y_send(c):
        return send(sy.at[c], ry.at[c], y_ssem.at[c], y_rsem.at[c], yhi)

    def c_send(c):
        return send(sc.at[c], rc.at[c], c_ssem.at[c], c_rsem.at[c], twin)

    def g_send(c, hb, b, slot, dev):
        piece = hid.at[c, hb, b]
        return send(piece, piece, g_ssem.at[c, slot], g_rsem.at[c, slot], dev)

    def l_send(c, h):
        return send(sl.at[c, h], rl.at[c, h], l_ssem.at[c, h], l_rsem.at[c, h], ylo)

    def during(it, lag, fn):
        t = 2 * (it - lag)

        @pl.when(jnp.logical_and(t > 0, t <= NZ))
        def _():
            fn(t - 1, chunk_of(t - 1))

        @pl.when(jnp.logical_and(t >= 0, t < NZ))
        def _():
            fn(t, chunk_of(t))

    def stage_arrive(t, c):
        step = (t + 1) // 2

        def take(lo, h, four):
            way = jnp.where(t == NZ - 1, four, 1 - lax.rem(t, 2))
            a_send(c, lo, h, way, step - 1).wait_recv()

            @pl.when(step < jnp.where(way == four, 4, 3))
            def _():
                a_send(c, lo, h, way, step).start()

        @pl.when(t > 0)
        def _():
            for h in range(2):
                take(0, h, 0)
                take(1, h, 1)

    def stage_first(t, c):
        lhs = jnp.concatenate([xs[c, :, h].reshape(96, half) for h in range(2)], axis=1)

        def put(o, part):
            for j in range(2):
                pf[c, 2 * o + j] = part[:, j * quarter : (j + 1) * quarter].reshape(2, 48, quarter)

        @pl.when(core == 0)
        def _():
            for o in range(2):
                put(o, nn(lhs, win[o]))

        @pl.when(core == 1)
        def _():
            for o in range(2):
                put(o, nt(lhs, wout[o]))

        for way in range(2):
            sx1[c, way] = pf[c, xat(2), way].astype(BF16)
            x1_send(c, way).start()
        for way in range(2):
            sx2[c, way, 1 - way] = pf[c, xat(2 * way - 1), 1 - way].astype(BF16)
            x2_send(c, way, 1 - way).start()

    def stage_x2(t, c):
        for way in range(2):
            x1_send(c, way).wait_recv()
            sx2[c, way, way] = (pf[c, xat(2 * way - 1), way] + rx1[c, way].astype(F32)).astype(BF16)
            x2_send(c, way, way).start()

    def stage_y(t, c):
        for way in range(2):
            for b in range(2):
                x2_send(c, way, b).wait_recv()
        sy[c] = (
            pf[c, x, 1 - yh] + rx2[c, 0, 1 - yh].astype(F32) + rx2[c, 1, 1 - yh].astype(F32)
        )
        y_send(c).start()

    def stage_twin(t, c):
        y_send(c).wait_recv()
        sc[c] = pf[c, x, yh] + rx2[c, 0, yh].astype(F32) + rx2[c, 1, yh].astype(F32) + ry[c]
        c_send(c).start()

    def stage_gelu(t, c):
        c_send(c).wait_recv()

        @pl.when(core == 0)
        def _():
            hid[c, x, yh] = (rc[c] * gelu_slope(sc[c])).astype(BF16)

        @pl.when(core == 1)
        def _():
            hid[c, x, yh] = gelu_value(rc[c]).astype(BF16)

        g_send(c, x, yh, 0, yhi).start()
        g_send(c, x, yh, 1 + yh, xdev(1)).start()
        g_send(c, x, yh, 3 + yh, xdev(-1)).start()

    def forward(c, b):
        slot = 1 + 2 * b + b
        hb = xat(2 * b - 1)
        g_send(c, hb, b, slot, yhi).wait_recv()
        g_send(c, hb, b, 5 + b, xdev(1 - 2 * b)).start()

    def stage_spread(t, c):
        g_send(c, x, 1 - yh, 0, yhi).wait_recv()
        g_send(c, x, 1 - yh, 2 - yh, xdev(1)).start()
        g_send(c, x, 1 - yh, 4 - yh, xdev(-1)).start()
        forward(c, yh)

    def stage_spread2(t, c):
        forward(c, 1 - yh)

    def stage_second(t, c):
        g_send(c, xat(-1), 1, 2, yhi).wait_recv()
        g_send(c, xat(1), 0, 3, yhi).wait_recv()
        for b in range(2):
            g_send(c, xat(2), b, 5 + b, yhi).wait_recv()
        lhs = [
            jnp.concatenate([hid[c, 2 * o + j].reshape(96, quarter) for j in range(2)], axis=1) for o in range(2)
        ]

        @pl.when(core == 0)
        def _():
            oacc[c] = (nt(lhs[0], win[0]) + nt(lhs[1], win[1])).reshape(2, 48, width)

        @pl.when(core == 1)
        def _():
            oacc[c] = (nn(lhs[0], wout[0]) + nn(lhs[1], wout[1])).reshape(2, 48, width)

        for h in range(2):
            if not REDUCE_BOTH[h]:
                sl[c, h] = oacc[c, 1 - yl, :, h * half : (h + 1) * half].astype(BF16)
                l_send(c, h).start()

    def stage_pair(t, c):
        for h in range(2):
            if not REDUCE_BOTH[h]:
                l_send(c, h).wait_recv()
                oacc[c, yl, :, h * half : (h + 1) * half] += rl[c, h].astype(F32)

    stages = ((stage_first, 0), (stage_y, 1), (stage_spread, 2), (stage_second, 3), (stage_x2, 0), (stage_twin, 1), (stage_spread2, 2), (stage_pair, 4), (stage_gelu, 1), (stage_arrive, -1))

    def loop(it, carry):
        for fn, lag in stages:
            during(it, lag, fn)
        return carry

    lax.fori_loop(0, NZ // 2 + 1 + LAST, loop, 0)

    def grad_tile(o, i):
        @pl.when(core == 0)
        def _():
            lhs = xs[:, :, i // 2, :, pl.ds(pl.multiple_of(lax.rem(i, 2) * quarter, 128), quarter)]
            lhs = lhs.reshape(NZ * 96, quarter)
            rhs = jnp.concatenate([hid[:, 2 * o + j].reshape(NZ * 96, quarter) for j in range(2)], axis=1)
            grads[o, i] = (tn(lhs, rhs) * scale).astype(BF16)

        @pl.when(core == 1)
        def _():
            lhs = hid[:, 2 * o + i // 2].reshape(NZ * 96, quarter)
            rhs = xs[:, :, lax.rem(i, 2)].reshape(NZ * 96, half)
            grads[o, i] = (tn(lhs, rhs) * scale).astype(BF16)

    def grad_place(i):
        a = wigrad.at[pl.ds(pl.multiple_of(i * quarter, 128), quarter), :]
        b = wograd.at[
            pl.ds(pl.multiple_of((i // 2) * quarter, 128), quarter),
            pl.ds(pl.multiple_of(lax.rem(i, 2) * half, 128), half),
        ]
        return a, b

    def grad_send(i):
        a, b = grad_place(i)

        @pl.when(core == 0)
        def _():
            send(grads.at[1, i], a, o_ssem.at[i], o_rsem.at[i], twin).start()

        @pl.when(core == 1)
        def _():
            send(grads.at[0, i], b, o_ssem.at[i], o_rsem.at[i], twin).start()

    def grad_keep(i):
        a, b = grad_place(i)

        @pl.when(core == 0)
        def _():
            pltpu.make_async_copy(grads.at[0, i], a, o_lsem.at[i]).start()

        @pl.when(core == 1)
        def _():
            pltpu.make_async_copy(grads.at[1, i], b, o_lsem.at[i]).start()

    def grad_step(k):
        def one(i, carry):
            if k < 2:
                grad_tile(other, i)
                grad_send(i)
            else:
                grad_tile(core, i)
                grad_keep(i)
            return carry

        first = 2 * (k % 2)
        lax.fori_loop(first, first + 2, one, 0)

    streams = []
    for h in range(2):
        for far in ((True, False) if REDUCE_BOTH[h] else (False,)):
            longer = 1 if (h == 0) == far else -1
            for sign in (1, -1):
                streams.append((sign, h, far, 4 if sign == longer else 3))
    order = sorted(range(len(streams)), key=lambda i: (not streams[i][2], -streams[i][3]))

    def target(far):
        return 1 - yl if far else yl

    def d_send(s, k):
        return send(sd.at[s, k], rd.at[s, k], d_ssem.at[s, k], d_rsem.at[s, k], zdev(streams[s][0]))

    def e_send(h):
        return send(se.at[h], re.at[h], e_ssem.at[h], e_rsem.at[h], ylo)

    def waits_for_pair(s):
        return streams[s][3] == 4 and not REDUCE_BOTH[streams[s][1]]

    order.sort(key=waits_for_pair)
    paired = False
    for k in range(4):
        for s in order:
            sign, h, far, hops = streams[s]
            if k >= hops:
                continue
            if waits_for_pair(s) and not paired:
                stage_pair(NZ - 1, chunk_of(NZ - 1))
                paired = True
            dest = lax.rem(z + NZ + sign * (hops - k), NZ)
            value = oacc[dest, target(far), :, h * half : (h + 1) * half]
            if k > 0:
                d_send(s, k - 1).wait_recv()
                value = value + rd[s, k - 1].astype(F32)
            sd[s, k] = value.astype(BF16)
            d_send(s, k).start()
        grad_step(k)

    def ring_total(h, far):
        value = oacc[z, target(far), :, h * half : (h + 1) * half]
        for s, (_, at, away, hops) in enumerate(streams):
            if at == h and away == far:
                d_send(s, hops - 1).wait_recv()
                value = value + rd[s, hops - 1].astype(F32)
        return value

    for h in range(2):
        if REDUCE_BOTH[h]:
            se[h] = ring_total(h, True)
            e_send(h).start()
    parts = [ring_total(h, False) for h in range(2)]
    for h in range(2):
        if REDUCE_BOTH[h]:
            e_send(h).wait_recv()
            parts[h] = parts[h] + re[h]
    total = jnp.concatenate(parts, axis=1)
    fin[0] = total[:24].astype(BF16)
    fin[1] = total[24:].astype(BF16)

    @pl.when(core == 0)
    def _():
        send(fin.at[1], igrad, f_ssem, f_rsem, twin).start()
        pltpu.make_async_copy(fin.at[0], igrad, f_lsem).start()

    @pl.when(core == 1)
    def _():
        send(fin.at[0], out, f_ssem, f_rsem, twin).start()
        pltpu.make_async_copy(fin.at[1], out, f_lsem).start()

    for way in range(2):
        for h in range(2):
            for lo, four in ((0, 0), (1, 1)):
                for step in range(4 if way == four else 3):
                    a_send(z, lo, h, way, step).wait_send()
    for h in range(2):
        if REDUCE_BOTH[h]:
            e_send(h).wait_send()

    def drain(c, carry):
        for way in range(2):
            x1_send(c, way).wait_send()
            for b in range(2):
                x2_send(c, way, b).wait_send()
        y_send(c).wait_send()
        c_send(c).wait_send()
        for slot in range(7):
            g_send(c, x, yh, slot, yhi).wait_send()
        for h in range(2):
            if not REDUCE_BOTH[h]:
                l_send(c, h).wait_send()
        return carry

    lax.fori_loop(0, NZ, drain, 0)
    for s in range(len(streams)):
        for k in range(streams[s][3]):
            d_send(s, k).wait_send()

    for c, mine, his, parcel, wbuf, slot, result, other_result, tokens in (
        (0, wigrad, wograd, weight_out, wout, 0, igrad, out, cotangent),
        (1, wograd, wigrad, weight_in, win, 1, out, igrad, inputs),
    ):
        @pl.when(core == c)
        def _():
            for k in range(3):
                send(tokens, xp.at[yl, c], xp_ssem.at[k], xp_rsem.at[k], twin).wait_send()
            send(parcel, wbuf.at[slot], w_ssem, w_rsem, twin).wait_send()
            for i in range(4):
                a, b = grad_place(i)
                keep, take = (a, b) if c == 0 else (b, a)
                pltpu.make_async_copy(grads.at[c, i], keep, o_lsem.at[i]).wait()
                send(grads.at[1 - c, i], keep, o_ssem.at[i], o_rsem.at[i], twin).wait_send()
                send(grads.at[c, i], take, o_ssem.at[i], o_rsem.at[i], twin).wait_recv()
            pltpu.make_async_copy(fin.at[c], result, f_lsem).wait()
            send(fin.at[1 - c], result, f_ssem, f_rsem, twin).wait_send()
            send(fin.at[c], other_result, f_ssem, f_rsem, twin).wait_recv()


def body(inputs, weight_in, weight_out, cotangent):
    tokens, width = inputs.shape
    hidden = weight_in.shape[1]
    quarter = width // 4
    total_tokens = tokens * 32
    dma = pltpu.SemaphoreType.DMA
    vmem = pltpu.VMEM
    piece = (48, quarter)
    scratch = [
        vmem((2, 2, tokens, width), BF16),
        vmem((NZ, 2, 2, 48, width // 2), BF16),
        vmem((2, width, hidden), BF16),
        vmem((2, hidden, width), BF16),
        vmem((NZ, 4, 2) + piece, F32),
        vmem((NZ, 2) + piece, BF16),
        vmem((NZ, 2) + piece, BF16),
        vmem((NZ, 2, 2) + piece, BF16),
        vmem((NZ, 2, 2) + piece, BF16),
        vmem((NZ,) + piece, F32),
        vmem((NZ,) + piece, F32),
        vmem((NZ,) + piece, F32),
        vmem((NZ,) + piece, F32),
        vmem((NZ, 4, 2) + piece, BF16),
        vmem((NZ, 2, 48, width), F32),
        vmem((NZ, 2, 48, width // 2), BF16),
        vmem((NZ, 2, 48, width // 2), BF16),
        vmem((8, 4, 48, width // 2), BF16),
        vmem((8, 4, 48, width // 2), BF16),
        vmem((2, 48, width // 2), F32),
        vmem((2, 48, width // 2), F32),
        vmem((2, 4, quarter, width // 2), BF16),
        vmem((2, tokens, width), BF16),
        dma((2,)),
        dma, dma, dma((3,)), dma((3,)),
        dma((2, 2, 2, 4)), dma((2, 2, 2, 4)),
        dma((NZ, 2)), dma((NZ, 2)),
        dma((NZ, 2, 2)), dma((NZ, 2, 2)),
        dma((NZ,)), dma((NZ,)),
        dma((NZ,)), dma((NZ,)),
        dma((NZ, 7)), dma((NZ, 7)),
        dma((NZ, 2)), dma((NZ, 2)),
        dma((8, 4)), dma((8, 4)),
        dma((2,)), dma((2,)),
        dma((4,)), dma((4,)), dma((4,)),
        dma, dma, dma,
    ]
    shapes = (inputs.shape, cotangent.shape, weight_in.shape, weight_out.shape)
    return pl.pallas_call(
        functools.partial(kernel, float(total_tokens) ** (-0.5)),
        out_shape=tuple(jax.ShapeDtypeStruct(s, BF16) for s in shapes),
        in_specs=[pl.BlockSpec(memory_space=pl.ANY)] * 4,
        out_specs=tuple([pl.BlockSpec(memory_space=pl.ANY)] * 4),
        scratch_shapes=scratch,
        compiler_params=pltpu.CompilerParams(
            collective_id=0, has_side_effects=True, vmem_limit_bytes=58 * 1024 * 1024
        ),
        name="block",
    )(inputs, weight_in, weight_out, cotangent)


def solution(mesh):
    in_specs = (P("col", "row"), P("row", "col"), P("col", "row"), P("col", "row"))
    out_specs = (P("col", "row"), P("col", "row"), P("row", "col"), P("col", "row"))
    return jax.shard_map(body, mesh=mesh, in_specs=in_specs, out_specs=out_specs, check_vma=False)
```

```python
import functools
import math

import jax
import jax.numpy as jnp
from jax import lax
from jax.experimental import pallas as pl
from jax.experimental.pallas import tpu as pltpu
from jax.sharding import PartitionSpec as P

NZ = 8
NX = 4
F32 = jnp.float32
BF16 = jnp.bfloat16
COEFF = math.sqrt(2.0 / math.pi)
LAST = 3
REDUCE_BOTH = (True, False)


def gelu_value(preact):
    inner = COEFF * (preact + 0.044715 * preact * preact * preact)
    return 0.5 * preact * (1.0 + jnp.tanh(inner))


def gelu_slope(preact):
    inner = COEFF * (preact + 0.044715 * preact * preact * preact)
    tangent = jnp.tanh(inner)
    return 0.5 * (1.0 + tangent) + 0.5 * preact * (1.0 - tangent * tangent) * COEFF * (
        1.0 + 3.0 * 0.044715 * preact * preact
    )


def nn(a, b):
    return lax.dot_general(a, b, (((1,), (0,)), ((), ())), preferred_element_type=F32)


def nt(a, b):
    return lax.dot_general(a, b, (((1,), (1,)), ((), ())), preferred_element_type=F32)


def tn(a, b):
    return lax.dot_general(a, b, (((0,), (0,)), ((), ())), preferred_element_type=F32)


def kernel(
    scale,
    inputs, weight_in, weight_out, cotangent,
    out, igrad, wigrad, wograd,
    xp, xs, win, wout, pf, sx1, rx1, sx2, rx2, sy, ry, sc, rc, hid, oacc, sl, rl, sd, rd, se, re, grads, fin,
    loc_sem, w_ssem, w_rsem, xp_ssem, xp_rsem, a_ssem, a_rsem,
    x1_ssem, x1_rsem, x2_ssem, x2_rsem, y_ssem, y_rsem, c_ssem, c_rsem, g_ssem, g_rsem,
    l_ssem, l_rsem, d_ssem, d_rsem, e_ssem, e_rsem, o_lsem, o_ssem, o_rsem, f_lsem, f_ssem, f_rsem,
):
    row, col = lax.axis_index("row"), lax.axis_index("col")
    x, yh = row // 2, lax.rem(row, 2)
    yl, z, core = col // 16, lax.rem(col // 2, NZ), lax.rem(col, 2)
    other = 1 - core
    width = inputs.shape[1]
    half = width // 2
    quarter = width // 4
    twin = (row, col + 1 - 2 * core)
    ylo = (row, (1 - yl) * 16 + z * 2 + core)
    yhi = (x * 2 + 1 - yh, col)
    ylo_twin = (row, (1 - yl) * 16 + z * 2 + other)

    def zdev(step):
        return (row, yl * 16 + lax.rem(z + step + NZ, NZ) * 2 + core)

    def xdev(step):
        return (lax.rem(x + step + NX, NX) * 2 + yh, col)

    def xat(step):
        return lax.rem(x + step + NX, NX)

    def send(src, dst, ssem, rsem, dev):
        return pltpu.make_async_remote_copy(
            src_ref=src, dst_ref=dst, send_sem=ssem, recv_sem=rsem,
            device_id=dev, device_id_type=pl.DeviceIdType.MESH,
        )

    @pl.when(core == 0)
    def _():
        pltpu.make_async_copy(weight_in, win.at[0], loc_sem.at[0]).start()
        pltpu.make_async_copy(inputs, xp.at[yl, 0], loc_sem.at[1]).start()

    @pl.when(core == 1)
    def _():
        pltpu.make_async_copy(weight_out, wout.at[1], loc_sem.at[0]).start()
        pltpu.make_async_copy(cotangent, xp.at[yl, 1], loc_sem.at[1]).start()

    barrier = pltpu.get_barrier_semaphore()
    for dev in (twin, ylo, ylo_twin, yhi, zdev(1), zdev(-1), xdev(1), xdev(-1)):
        pl.semaphore_signal(barrier, inc=1, device_id=dev, device_id_type=pl.DeviceIdType.MESH)
    pl.semaphore_wait(barrier, 8)

    def token_sends(c, mine, his):
        slot = xp.at[yl, c]
        return (
            send(mine, slot, xp_ssem.at[1], xp_rsem.at[1], ylo),
            send(his, slot, xp_ssem.at[2], xp_rsem.at[2], ylo_twin),
            send(his, slot, xp_ssem.at[0], xp_rsem.at[0], twin),
        )

    @pl.when(core == 0)
    def _():
        for copy in token_sends(0, inputs, cotangent):
            copy.start()
        send(weight_out, wout.at[0], w_ssem, w_rsem, twin).start()

    @pl.when(core == 1)
    def _():
        for copy in token_sends(1, cotangent, inputs):
            copy.start()
        send(weight_in, win.at[1], w_ssem, w_rsem, twin).start()

    @pl.when(core == 0)
    def _():
        pltpu.make_async_copy(inputs, xp.at[yl, 0], loc_sem.at[1]).wait()

    @pl.when(core == 1)
    def _():
        pltpu.make_async_copy(cotangent, xp.at[yl, 1], loc_sem.at[1]).wait()

    def build(lo):
        block = jnp.concatenate([xp[lo, 0].astype(F32), xp[lo, 1].astype(F32)], axis=0).astype(BF16)
        for h in range(2):
            xs[z, lo, h] = block[:, h * half : (h + 1) * half]

    def a_send(chunk, lo, h, way, step):
        piece = xs.at[chunk, lo, h]
        dev = (row, yl * 16 + lax.rem(z + 1 - 2 * way + NZ, NZ) * 2 + core)
        return send(piece, piece, a_ssem.at[way, lo, h, step], a_rsem.at[way, lo, h, step], dev)

    send(inputs, xp.at[yl, other], xp_ssem.at[0], xp_rsem.at[0], twin).wait_recv()
    build(yl)
    for h in range(2):
        for way in range(2):
            a_send(z, yl, h, way, 0).start()
    send(inputs, xp.at[1 - yl, core], xp_ssem.at[1], xp_rsem.at[1], ylo).wait_recv()
    send(inputs, xp.at[1 - yl, other], xp_ssem.at[2], xp_rsem.at[2], ylo_twin).wait_recv()
    build(1 - yl)
    for h in range(2):
        for way in range(2):
            a_send(z, 1 - yl, h, way, 0).start()

    @pl.when(core == 0)
    def _():
        pltpu.make_async_copy(weight_in, win.at[0], loc_sem.at[0]).wait()
        send(weight_in, win.at[1], w_ssem, w_rsem, twin).wait_recv()

    @pl.when(core == 1)
    def _():
        pltpu.make_async_copy(weight_out, wout.at[1], loc_sem.at[0]).wait()
        send(weight_out, wout.at[0], w_ssem, w_rsem, twin).wait_recv()

    def chunk_of(t):
        step = (t + 1) // 2
        return lax.rem(z + NZ + (1 - 2 * lax.rem(t, 2)) * step, NZ)

    def x1_send(c, way):
        return send(sx1.at[c, way], rx1.at[c, way], x1_ssem.at[c, way], x1_rsem.at[c, way], xdev(2 * way - 1))

    def x2_send(c, way, b):
        return send(
            sx2.at[c, way, b], rx2.at[c, way, b], x2_ssem.at[c, way, b], x2_rsem.at[c, way, b], xdev(2 * way - 1)
        )

    def y_send(c):
        return send(sy.at[c], ry.at[c], y_ssem.at[c], y_rsem.at[c], yhi)

    def c_send(c):
        return send(sc.at[c], rc.at[c], c_ssem.at[c], c_rsem.at[c], twin)

    def g_send(c, hb, b, slot, dev):
        piece = hid.at[c, hb, b]
        return send(piece, piece, g_ssem.at[c, slot], g_rsem.at[c, slot], dev)

    def l_send(c, h):
        return send(sl.at[c, h], rl.at[c, h], l_ssem.at[c, h], l_rsem.at[c, h], ylo)

    def during(it, lag, fn):
        t = 2 * (it - lag)

        @pl.when(jnp.logical_and(t > 0, t <= NZ))
        def _():
            fn(t - 1, chunk_of(t - 1))

        @pl.when(jnp.logical_and(t >= 0, t < NZ))
        def _():
            fn(t, chunk_of(t))

    def stage_arrive(t, c):
        step = (t + 1) // 2

        def take(lo, h, four):
            way = jnp.where(t == NZ - 1, four, 1 - lax.rem(t, 2))
            a_send(c, lo, h, way, step - 1).wait_recv()

            @pl.when(step < jnp.where(way == four, 4, 3))
            def _():
                a_send(c, lo, h, way, step).start()

        @pl.when(t > 0)
        def _():
            for h in range(2):
                take(0, h, 0)
                take(1, h, 1)

    def stage_first(t, c):
        lhs = jnp.concatenate([xs[c, :, h].reshape(96, half) for h in range(2)], axis=1)

        def put(o, part):
            for j in range(2):
                pf[c, 2 * o + j] = part[:, j * quarter : (j + 1) * quarter].reshape(2, 48, quarter)

        @pl.when(core == 0)
        def _():
            for o in range(2):
                put(o, nn(lhs, win[o]))

        @pl.when(core == 1)
        def _():
            for o in range(2):
                put(o, nt(lhs, wout[o]))

        for way in range(2):
            sx1[c, way] = pf[c, xat(2), way].astype(BF16)
            x1_send(c, way).start()
        for way in range(2):
            sx2[c, way, 1 - way] = pf[c, xat(2 * way - 1), 1 - way].astype(BF16)
            x2_send(c, way, 1 - way).start()

    def stage_x2(t, c):
        for way in range(2):
            x1_send(c, way).wait_recv()
            sx2[c, way, way] = (pf[c, xat(2 * way - 1), way] + rx1[c, way].astype(F32)).astype(BF16)
            x2_send(c, way, way).start()

    def stage_y(t, c):
        for way in range(2):
            for b in range(2):
                x2_send(c, way, b).wait_recv()
        sy[c] = (
            pf[c, x, 1 - yh] + rx2[c, 0, 1 - yh].astype(F32) + rx2[c, 1, 1 - yh].astype(F32)
        )
        y_send(c).start()

    def stage_twin(t, c):
        y_send(c).wait_recv()
        sc[c] = pf[c, x, yh] + rx2[c, 0, yh].astype(F32) + rx2[c, 1, yh].astype(F32) + ry[c]
        c_send(c).start()

    def stage_gelu(t, c):
        c_send(c).wait_recv()

        @pl.when(core == 0)
        def _():
            hid[c, x, yh] = (rc[c] * gelu_slope(sc[c])).astype(BF16)

        @pl.when(core == 1)
        def _():
            hid[c, x, yh] = gelu_value(rc[c]).astype(BF16)

        g_send(c, x, yh, 0, yhi).start()
        g_send(c, x, yh, 1 + yh, xdev(1)).start()
        g_send(c, x, yh, 3 + yh, xdev(-1)).start()

    def forward(c, b):
        slot = 1 + 2 * b + b
        hb = xat(2 * b - 1)
        g_send(c, hb, b, slot, yhi).wait_recv()
        g_send(c, hb, b, 5 + b, xdev(1 - 2 * b)).start()

    def stage_spread(t, c):
        g_send(c, x, 1 - yh, 0, yhi).wait_recv()
        g_send(c, x, 1 - yh, 2 - yh, xdev(1)).start()
        g_send(c, x, 1 - yh, 4 - yh, xdev(-1)).start()
        forward(c, yh)

    def stage_spread2(t, c):
        forward(c, 1 - yh)

    def stage_second(t, c):
        g_send(c, xat(-1), 1, 2, yhi).wait_recv()
        g_send(c, xat(1), 0, 3, yhi).wait_recv()
        for b in range(2):
            g_send(c, xat(2), b, 5 + b, yhi).wait_recv()
        lhs = [
            jnp.concatenate([hid[c, 2 * o + j].reshape(96, quarter) for j in range(2)], axis=1) for o in range(2)
        ]

        @pl.when(core == 0)
        def _():
            oacc[c] = (nt(lhs[0], win[0]) + nt(lhs[1], win[1])).reshape(2, 48, width)

        @pl.when(core == 1)
        def _():
            oacc[c] = (nn(lhs[0], wout[0]) + nn(lhs[1], wout[1])).reshape(2, 48, width)

        for h in range(2):
            if not REDUCE_BOTH[h]:
                sl[c, h] = oacc[c, 1 - yl, :, h * half : (h + 1) * half].astype(BF16)
                l_send(c, h).start()

    def stage_pair(t, c):
        for h in range(2):
            if not REDUCE_BOTH[h]:
                l_send(c, h).wait_recv()
                oacc[c, yl, :, h * half : (h + 1) * half] += rl[c, h].astype(F32)

    stages = ((stage_first, 0), (stage_y, 1), (stage_spread, 2), (stage_second, 3), (stage_x2, 0), (stage_twin, 1), (stage_spread2, 2), (stage_pair, 4), (stage_gelu, 1), (stage_arrive, -1))

    def loop(it, carry):
        for fn, lag in stages:
            during(it, lag, fn)
        return carry

    lax.fori_loop(0, NZ // 2 + 1 + LAST, loop, 0)

    def grad_tile(o, i):
        @pl.when(core == 0)
        def _():
            lhs = xs[:, :, i // 2, :, pl.ds(pl.multiple_of(lax.rem(i, 2) * quarter, 128), quarter)]
            lhs = lhs.reshape(NZ * 96, quarter)
            rhs = jnp.concatenate([hid[:, 2 * o + j].reshape(NZ * 96, quarter) for j in range(2)], axis=1)
            grads[o, i] = (tn(lhs, rhs) * scale).astype(BF16)

        @pl.when(core == 1)
        def _():
            lhs = hid[:, 2 * o + i // 2].reshape(NZ * 96, quarter)
            rhs = xs[:, :, lax.rem(i, 2)].reshape(NZ * 96, half)
            grads[o, i] = (tn(lhs, rhs) * scale).astype(BF16)

    def grad_place(i):
        a = wigrad.at[pl.ds(pl.multiple_of(i * quarter, 128), quarter), :]
        b = wograd.at[
            pl.ds(pl.multiple_of((i // 2) * quarter, 128), quarter),
            pl.ds(pl.multiple_of(lax.rem(i, 2) * half, 128), half),
        ]
        return a, b

    def grad_send(i):
        a, b = grad_place(i)

        @pl.when(core == 0)
        def _():
            send(grads.at[1, i], a, o_ssem.at[i], o_rsem.at[i], twin).start()

        @pl.when(core == 1)
        def _():
            send(grads.at[0, i], b, o_ssem.at[i], o_rsem.at[i], twin).start()

    def grad_keep(i):
        a, b = grad_place(i)

        @pl.when(core == 0)
        def _():
            pltpu.make_async_copy(grads.at[0, i], a, o_lsem.at[i]).start()

        @pl.when(core == 1)
        def _():
            pltpu.make_async_copy(grads.at[1, i], b, o_lsem.at[i]).start()

    def grad_step(k):
        def one(i, carry):
            if k < 2:
                grad_tile(other, i)
                grad_send(i)
            else:
                grad_tile(core, i)
                grad_keep(i)
            return carry

        first = 2 * (k % 2)
        lax.fori_loop(first, first + 2, one, 0)

    streams = []
    for h in range(2):
        for far in ((True, False) if REDUCE_BOTH[h] else (False,)):
            longer = 1 if (h == 0) == far else -1
            for sign in (1, -1):
                streams.append((sign, h, far, 4 if sign == longer else 3))
    order = sorted(range(len(streams)), key=lambda i: (not streams[i][2], -streams[i][3]))

    def target(far):
        return 1 - yl if far else yl

    def d_send(s, k):
        return send(sd.at[s, k], rd.at[s, k], d_ssem.at[s, k], d_rsem.at[s, k], zdev(streams[s][0]))

    def e_send(h):
        return send(se.at[h], re.at[h], e_ssem.at[h], e_rsem.at[h], ylo)

    def waits_for_pair(s):
        return streams[s][3] == 4 and not REDUCE_BOTH[streams[s][1]]

    order.sort(key=waits_for_pair)
    paired = False
    for k in range(4):
        for s in order:
            sign, h, far, hops = streams[s]
            if k >= hops:
                continue
            if waits_for_pair(s) and not paired:
                stage_pair(NZ - 1, chunk_of(NZ - 1))
                paired = True
            dest = lax.rem(z + NZ + sign * (hops - k), NZ)
            value = oacc[dest, target(far), :, h * half : (h + 1) * half]
            if k > 0:
                d_send(s, k - 1).wait_recv()
                value = value + rd[s, k - 1].astype(F32)
            sd[s, k] = value.astype(BF16)
            d_send(s, k).start()
        grad_step(k)

    def ring_total(h, far):
        value = oacc[z, target(far), :, h * half : (h + 1) * half]
        for s, (_, at, away, hops) in enumerate(streams):
            if at == h and away == far:
                d_send(s, hops - 1).wait_recv()
                value = value + rd[s, hops - 1].astype(F32)
        return value

    for h in range(2):
        if REDUCE_BOTH[h]:
            se[h] = ring_total(h, True)
            e_send(h).start()
    parts = [ring_total(h, False) for h in range(2)]
    for h in range(2):
        if REDUCE_BOTH[h]:
            e_send(h).wait_recv()
            parts[h] = parts[h] + re[h]
    total = jnp.concatenate(parts, axis=1)
    fin[0] = total[:24].astype(BF16)
    fin[1] = total[24:].astype(BF16)

    @pl.when(core == 0)
    def _():
        send(fin.at[1], igrad, f_ssem, f_rsem, twin).start()
        pltpu.make_async_copy(fin.at[0], igrad, f_lsem).start()

    @pl.when(core == 1)
    def _():
        send(fin.at[0], out, f_ssem, f_rsem, twin).start()
        pltpu.make_async_copy(fin.at[1], out, f_lsem).start()

    for way in range(2):
        for h in range(2):
            for lo, four in ((0, 0), (1, 1)):
                for step in range(4 if way == four else 3):
                    a_send(z, lo, h, way, step).wait_send()
    for h in range(2):
        if REDUCE_BOTH[h]:
            e_send(h).wait_send()

    def drain(c, carry):
        for way in range(2):
            x1_send(c, way).wait_send()
            for b in range(2):
                x2_send(c, way, b).wait_send()
        y_send(c).wait_send()
        c_send(c).wait_send()
        for slot in range(7):
            g_send(c, x, yh, slot, yhi).wait_send()
        for h in range(2):
            if not REDUCE_BOTH[h]:
                l_send(c, h).wait_send()
        return carry

    lax.fori_loop(0, NZ, drain, 0)
    for s in range(len(streams)):
        for k in range(streams[s][3]):
            d_send(s, k).wait_send()

    for c, mine, his, parcel, wbuf, slot, result, other_result, tokens in (
        (0, wigrad, wograd, weight_out, wout, 0, igrad, out, cotangent),
        (1, wograd, wigrad, weight_in, win, 1, out, igrad, inputs),
    ):
        @pl.when(core == c)
        def _():
            for k in range(3):
                send(tokens, xp.at[yl, c], xp_ssem.at[k], xp_rsem.at[k], twin).wait_send()
            send(parcel, wbuf.at[slot], w_ssem, w_rsem, twin).wait_send()
            for i in range(4):
                a, b = grad_place(i)
                keep, take = (a, b) if c == 0 else (b, a)
                pltpu.make_async_copy(grads.at[c, i], keep, o_lsem.at[i]).wait()
                send(grads.at[1 - c, i], keep, o_ssem.at[i], o_rsem.at[i], twin).wait_send()
                send(grads.at[c, i], take, o_ssem.at[i], o_rsem.at[i], twin).wait_recv()
            pltpu.make_async_copy(fin.at[c], result, f_lsem).wait()
            send(fin.at[1 - c], result, f_ssem, f_rsem, twin).wait_send()
            send(fin.at[c], other_result, f_ssem, f_rsem, twin).wait_recv()


def body(inputs, weight_in, weight_out, cotangent):
    tokens, width = inputs.shape
    hidden = weight_in.shape[1]
    quarter = width // 4
    total_tokens = tokens * 32
    dma = pltpu.SemaphoreType.DMA
    vmem = pltpu.VMEM
    piece = (48, quarter)
    scratch = [
        vmem((2, 2, tokens, width), BF16),
        vmem((NZ, 2, 2, 48, width // 2), BF16),
        vmem((2, width, hidden), BF16),
        vmem((2, hidden, width), BF16),
        vmem((NZ, 4, 2) + piece, F32),
        vmem((NZ, 2) + piece, BF16),
        vmem((NZ, 2) + piece, BF16),
        vmem((NZ, 2, 2) + piece, BF16),
        vmem((NZ, 2, 2) + piece, BF16),
        vmem((NZ,) + piece, F32),
        vmem((NZ,) + piece, F32),
        vmem((NZ,) + piece, F32),
        vmem((NZ,) + piece, F32),
        vmem((NZ, 4, 2) + piece, BF16),
        vmem((NZ, 2, 48, width), F32),
        vmem((NZ, 2, 48, width // 2), BF16),
        vmem((NZ, 2, 48, width // 2), BF16),
        vmem((8, 4, 48, width // 2), BF16),
        vmem((8, 4, 48, width // 2), BF16),
        vmem((2, 48, width // 2), F32),
        vmem((2, 48, width // 2), F32),
        vmem((2, 4, quarter, width // 2), BF16),
        vmem((2, tokens, width), BF16),
        dma((2,)),
        dma, dma, dma((3,)), dma((3,)),
        dma((2, 2, 2, 4)), dma((2, 2, 2, 4)),
        dma((NZ, 2)), dma((NZ, 2)),
        dma((NZ, 2, 2)), dma((NZ, 2, 2)),
        dma((NZ,)), dma((NZ,)),
        dma((NZ,)), dma((NZ,)),
        dma((NZ, 7)), dma((NZ, 7)),
        dma((NZ, 2)), dma((NZ, 2)),
        dma((8, 4)), dma((8, 4)),
        dma((2,)), dma((2,)),
        dma((4,)), dma((4,)), dma((4,)),
        dma, dma, dma,
    ]
    shapes = (inputs.shape, cotangent.shape, weight_in.shape, weight_out.shape)
    return pl.pallas_call(
        functools.partial(kernel, float(total_tokens) ** (-0.5)),
        out_shape=tuple(jax.ShapeDtypeStruct(s, BF16) for s in shapes),
        in_specs=[pl.BlockSpec(memory_space=pl.ANY)] * 4,
        out_specs=tuple([pl.BlockSpec(memory_space=pl.ANY)] * 4),
        scratch_shapes=scratch,
        compiler_params=pltpu.CompilerParams(
            collective_id=0, has_side_effects=True, vmem_limit_bytes=58 * 1024 * 1024
        ),
        name="block",
    )(inputs, weight_in, weight_out, cotangent)


def solution(mesh):
    in_specs = (P("col", "row"), P("row", "col"), P("col", "row"), P("col", "row"))
    out_specs = (P("col", "row"), P("col", "row"), P("row", "col"), P("col", "row"))
    return jax.shard_map(body, mesh=mesh, in_specs=in_specs, out_specs=out_specs, check_vma=False)
```
